256 devices in a mesh: dp: 64 (over z, x, y_hi), ctx: 4 (over y_lo, core).
Axes of the slice: x: 4, y: 4 (y_hi: 2, y_lo: 2; y = y_hi * 2 + y_lo), z: 8, core: 2. Of those that a mesh axis runs over, the one named last changes fastest.
Arguments:
- queries: bfloat16 [192, 128, 576], P('dp', 'ctx'), may hold values from -25 to 25
- latent_cache: bfloat16 [192, 12800, 576], P('dp', 'ctx'), may hold values from -15 to 15
- lengths: int32 [192], P('dp'), may hold values from 2 to 12800, as said below
- value_up_matrix: bfloat16 [128, 512, 128], P('dp'), may hold values from -1.5 to 1.5
- out_weight: bfloat16 [16384, 7168], P('dp', 'ctx'), may hold values from -0.046875 to 0.046875
Outputs:
- layer_out: bfloat16 [192, 7168], P('dp', 'ctx')
The draws below stay inside these ranges and needn't reach their ends.
Inputs may be any that keep to these rules, and one draw needn't show every extreme that they name: `lengths`: each row has 2 or more live positions; some row has all 12800.
All inputs are finite; a program needn't handle non-finite values.
Results may differ from the reference program's by a relative error of at most 0.022.
Values may be sent and summed in bfloat16 or wider, within the bound.
No kernel may reach another device: no remote copies, remote signals or barrier semaphores. Data moves between devices by JAX's collectives and lax.ppermute only.
A program may use at most 64 MiB of HBM per device.

```python
import jax
import jax.numpy as jnp
from jax import lax

H = 128
LAT = 512
ROPE = 64
QK = 128
VH = 128
D = 7168
B = 192
LMAX = 12800


def draw_queries(key, part):
    key = jax.random.fold_in(key, 1)
    return jnp.clip(jax.random.normal(key, (B, H, LAT + ROPE), jnp.float32), -6.0, 6.0).astype(jnp.bfloat16)


def draw_latent_cache(key, part):
    key = jax.random.fold_in(key, 2)
    return jnp.clip(jax.random.normal(key, (B, LMAX, LAT + ROPE), jnp.float32), -6.0, 6.0).astype(jnp.bfloat16)


def draw_lengths(key, part):
    key = jax.random.fold_in(key, 3)
    values = jax.random.randint(key, (B,), 2, LMAX + 1)
    longest = jax.random.randint(jax.random.fold_in(key, 4), (), 0, B)
    return values.at[longest].set(LMAX).astype(jnp.int32)


def levels(rng, dims, cuts, low, largest):
    def one(position, blocks):
        heights = jax.random.uniform(jax.random.fold_in(jax.random.fold_in(rng, 6), position), (blocks,), jnp.float32, low / len(cuts), largest / len(cuts))
        return jnp.repeat(jnp.exp(heights), dims[position] // blocks).reshape((-1,) + (1,) * (len(dims) - position - 1))

    gain = one(*cuts[0])
    for cut in cuts[1:]:
        gain = gain * one(*cut)
    return gain


def gaussian(own_key, extent, deviation, most, pieces=(), held_as=jnp.bfloat16):
    values = deviation * jax.random.normal(own_key, extent, jnp.float32)
    if pieces:
        values = values * levels(own_key, extent, pieces, -0.22, 0.18)
    return jnp.clip(values, -most, most).astype(held_as)


def setup_inputs(seed: int = 0) -> dict:
    arg_keys = jax.random.split(jax.random.key(seed), 6)
    return {
        "queries": draw_queries(jax.random.fold_in(arg_keys[5], 71), 0),
        "latent_cache": draw_latent_cache(jax.random.fold_in(arg_keys[5], 71), 0),
        "lengths": draw_lengths(jax.random.fold_in(arg_keys[5], 71), 0),
        "value_up_matrix": gaussian(arg_keys[3], (H, LAT, VH), 0.25, 1.5, ((0, 64),)),
        "out_weight": gaussian(arg_keys[4], (H * VH, D), (H * VH) ** -0.5, 0.046875, ((0, 64), (1, 4))),
    }


def attend_row(inputs):
    query_row, cache_row, length_row = inputs
    score_scale = (QK + ROPE) ** -0.5
    scores = jnp.dot(query_row, cache_row.T, preferred_element_type=jnp.float32) * score_scale
    live_mask = (lax.iota(jnp.int32, LMAX) < length_row)[None, :]
    scores = jnp.where(live_mask, scores, -1e30)
    row_peak = jnp.max(scores, axis=1, keepdims=True)
    weights = jnp.where(live_mask, jnp.exp(scores - row_peak), 0.0)
    row_total = jnp.sum(weights, axis=1)
    mixed = jnp.dot(weights.astype(jnp.bfloat16), cache_row[:, :LAT], preferred_element_type=jnp.float32)
    return (mixed / row_total[:, None]).astype(jnp.bfloat16)


def reference(queries, latent_cache, lengths, value_up_matrix, out_weight):
    latent_result = lax.map(attend_row, (queries, latent_cache, lengths))
    head_result = jnp.einsum("rod,odm->rom", latent_result.astype(jnp.float32), value_up_matrix.astype(jnp.float32)).astype(jnp.bfloat16)
    flat_heads = head_result.reshape(B, H * VH)
    return jnp.dot(flat_heads, out_weight, preferred_element_type=jnp.float32).astype(jnp.bfloat16)
```

```python
import functools

import jax
import jax.numpy as jnp
import numpy as np
from jax import lax
from jax.experimental import pallas as pl
from jax.experimental.pallas import tpu as pltpu
from jax.sharding import Mesh, PartitionSpec as P

ROPE = 64
QK = 128
SCALE = (QK + ROPE) ** -0.5
DEAD = -1e30
DP = ("z", "x", "yh")
CTX = ("yl", "core")
STAT_ROWS = 16
VMEM = pl.BlockSpec(memory_space=pltpu.VMEM)
SMEM = pl.BlockSpec(memory_space=pltpu.SMEM)


def product(a, b, dim_a, dim_b):
    return lax.dot_general(
        a, b, (((dim_a,), (dim_b,)), ((), ())), preferred_element_type=jnp.float32
    )


def attend_kernel(rows, heads, lat, query_ref, cache_ref, length_ref, out_ref, stat_ref):
    row = pl.program_id(0)
    scores = product(query_ref[0], cache_ref[0], 1, 0) * SCALE
    positions = lax.broadcasted_iota(jnp.int32, scores.shape, 1)
    scores = jnp.where(positions < length_ref[row], scores, DEAD)
    peak = jnp.max(scores, axis=1, keepdims=True)
    weights = jnp.exp(scores - peak)
    total = jnp.sum(weights, axis=1, keepdims=True)
    mixed = product(weights.astype(jnp.bfloat16), cache_ref[0, :lat], 1, 1)
    mixed = (mixed / total).astype(jnp.bfloat16)
    quarters = out_ref.shape[0]
    width = lat // quarters
    place = pl.ds(pl.multiple_of(row * heads, heads), heads)
    for k in range(quarters):
        out_ref[k, place, :] = mixed[:, k * width : (k + 1) * width]
    logsum = jnp.broadcast_to(peak + jnp.log(total), (heads, heads)).T[0:1]
    high = logsum.astype(jnp.bfloat16).astype(jnp.float32)
    middle = (logsum - high).astype(jnp.bfloat16).astype(jnp.float32)
    low = logsum - high - middle

    @pl.when(row == 0)
    def _():
        stat_ref[...] = jnp.zeros_like(stat_ref)

    stat_ref[pl.ds(3 * row, 1), :] = high
    stat_ref[pl.ds(3 * row + 1, 1), :] = middle
    stat_ref[pl.ds(3 * row + 2, 1), :] = low

    @pl.when(row == rows - 1)
    def _():
        for k in range(quarters):
            out_ref[k, rows * heads :, :] = stat_ref[...].astype(jnp.bfloat16)


def attend(queries, cache, lengths, lat, quarters):
    rows, heads, width = queries.shape
    span = cache.shape[2]
    shape = (quarters, rows * heads + STAT_ROWS, lat // quarters)
    return pl.pallas_call(
        functools.partial(attend_kernel, rows, heads, lat),
        grid=(rows,),
        in_specs=[
            pl.BlockSpec((1, heads, width), lambda i: (i, 0, 0)),
            pl.BlockSpec((1, width, span), lambda i: (i, 0, 0)),
            SMEM,
        ],
        out_specs=pl.BlockSpec(shape, lambda i: (0, 0, 0)),
        out_shape=jax.ShapeDtypeStruct(shape, jnp.bfloat16),
        scratch_shapes=[pltpu.VMEM((STAT_ROWS, heads), jnp.float32)],
        compiler_params=pltpu.CompilerParams(vmem_limit_bytes=48 << 20),
        name="attend",
    )(queries, cache, lengths)


def combine_kernel(rows, heads, part_ref, order_ref, out_ref):
    parts = part_ref.shape[0]
    stats = [part_ref[c, rows * heads :, :].astype(jnp.float32) for c in range(parts)]
    shares = []
    for row in range(rows):
        logsums = [s[3 * row : 3 * row + 1] + s[3 * row + 1 : 3 * row + 2] + s[3 * row + 2 : 3 * row + 3] for s in stats]
        peak = functools.reduce(jnp.maximum, logsums)
        factors = [jnp.exp(v - peak) for v in logsums]
        total = functools.reduce(jnp.add, factors)
        shares += [f / total for f in factors]
    shares.append(jnp.zeros((heads - len(shares), heads), jnp.float32))
    shares = jnp.concatenate(shares, axis=0).T
    merged = []
    for row in range(rows):
        total = None
        for c in range(parts):
            column = row * parts + c
            term = shares[:, column : column + 1] * part_ref[c, row * heads : (row + 1) * heads, :].astype(jnp.float32)
            total = term if total is None else total + term
        merged.append(total.astype(jnp.bfloat16))
    merged = jnp.concatenate(merged, axis=0)
    out_ref[...] = product(order_ref[...], merged, 1, 0).astype(jnp.bfloat16)


def combine(parts, order, rows, heads):
    return pl.pallas_call(
        functools.partial(combine_kernel, rows, heads),
        in_specs=[VMEM, VMEM],
        out_specs=VMEM,
        out_shape=jax.ShapeDtypeStruct((order.shape[0], parts.shape[2]), jnp.bfloat16),
        compiler_params=pltpu.CompilerParams(vmem_limit_bytes=32 << 20),
        name="combine",
    )(parts, order)


def project_kernel(owned, latent_ref, up_ref, select_ref, weight_ref, out_ref):
    latents = jnp.concatenate([latent_ref[k] for k in range(latent_ref.shape[0])], axis=1)
    ups = jnp.concatenate([up_ref[o] for o in range(owned)], axis=1)
    heads_out = product(latents, ups, 1, 0)
    slot = lax.broadcasted_iota(jnp.int32, heads_out.shape, 0) % 8
    column = lax.broadcasted_iota(jnp.int32, heads_out.shape, 1)
    mine = (slot // 4) == (column // up_ref.shape[2])
    heads_out = jnp.where(mine, heads_out, 0.0).astype(jnp.bfloat16)
    flat = product(select_ref[...], heads_out, 1, 0).astype(jnp.bfloat16)
    out_ref[...] = product(flat, weight_ref[...], 1, 0).astype(jnp.bfloat16)


def project(latents, ups, select, weight):
    return pl.pallas_call(
        functools.partial(project_kernel, ups.shape[0]),
        in_specs=[VMEM] * 4,
        out_specs=VMEM,
        out_shape=jax.ShapeDtypeStruct((select.shape[0], weight.shape[1]), jnp.bfloat16),
        compiler_params=pltpu.CompilerParams(vmem_limit_bytes=32 << 20),
        name="project",
    )(latents, ups, select, weight)


def shards(queries, cache, lengths, ups, weight):
    rows = queries.shape[0]
    owned, lat, _ = ups.shape
    z, x, yh = (lax.axis_size(a) for a in DP)
    near = x * yh
    owners = z * near
    groups = lax.axis_size(CTX[0]) * lax.axis_size(CTX[1])
    heads = queries.shape[1] * groups
    span = cache.shape[1]
    context = lax.axis_index(CTX)

    all_queries = lax.all_gather(queries, CTX, axis=1, tiled=True)
    parts = attend(all_queries, jnp.swapaxes(cache, 1, 2), lengths - context * span, lat, groups)
    parts = lax.all_to_all(parts, CTX, 0, 0, tiled=True)

    order = np.zeros((owners, 8, rows, owners, owned), np.float32)
    for d in range(owners):
        for o in range(owned):
            for i in range(rows):
                order[d, 4 * o + i, i, d, o] = 1
    order = jnp.asarray(order.reshape(owners * 8, rows * heads), jnp.bfloat16)
    merged = combine(parts, order, rows, heads).reshape(owners, 8, lat // groups)

    latents = lax.all_to_all(merged, DP, 0, 0, tiled=True)
    latents = lax.all_gather(latents, CTX, axis=0, tiled=False)
    latents = latents.reshape(groups, owners * 8, lat // groups)

    select = np.zeros((near, z, rows, z, near, 8), np.float32)
    for a in range(near):
        for b in range(z):
            for i in range(rows):
                for o in range(owned):
                    select[a, b, i, b, a, 4 * o + i] = 1
    select = jnp.asarray(select.reshape(owners * rows, owners * 8), jnp.bfloat16)
    partial = project(latents, ups, select, weight)

    width = weight.shape[1]
    partial = partial.reshape(near, z * rows, width)
    partial = lax.all_to_all(partial, DP[1:], 0, 0, tiled=True)
    partial = jnp.sum(partial.astype(jnp.float32), axis=0).astype(jnp.bfloat16)
    partial = lax.all_to_all(partial.reshape(z, rows, width), DP[0], 0, 0, tiled=True)
    return jnp.sum(partial.astype(jnp.float32), axis=0).astype(jnp.bfloat16)


def solution(mesh):
    inner = Mesh(mesh.devices.reshape(8, 4, 2, 2, 2), DP + CTX)
    return jax.shard_map(
        shards,
        mesh=inner,
        in_specs=(
            P(DP, CTX, None),
            P(DP, CTX, None),
            P(DP),
            P(DP, None, None),
            P(DP, CTX),
        ),
        out_specs=P(DP, CTX),
        check_vma=False,
    )
```

```python
import functools
import math

import jax
import jax.numpy as jnp
import numpy as np
from jax import lax
from jax.experimental import pallas as pl
from jax.experimental.pallas import tpu as pltpu
from jax.sharding import Mesh, PartitionSpec as P

ROPE = 64
QK = 128
SCALE = (QK + ROPE) ** -0.5
LOG2E = math.log2(math.e)
DEAD = -1e30
DP = ("z", "x", "yh")
PEERS = ("z", "yh")
CTX = ("yl", "core")
STAT_ROWS = 16
SLOTS = 4
VMEM = pl.BlockSpec(memory_space=pltpu.VMEM)
SMEM = pl.BlockSpec(memory_space=pltpu.SMEM)
ANY = pl.BlockSpec(memory_space=pl.ANY)


def product(a, b, dim_a, dim_b):
    return lax.dot_general(
        a, b, (((dim_a,), (dim_b,)), ((), ())), preferred_element_type=jnp.float32
    )


def swap(block, axis):
    return lax.ppermute(block, axis, [(0, 1), (1, 0)])


def call(kernel, name, out_shape, in_specs, scratch=(), out_specs=None, vmem=24, work=0):
    return pl.pallas_call(
        kernel,
        in_specs=in_specs,
        out_specs=jax.tree.map(lambda _: VMEM, out_shape) if out_specs is None else out_specs,
        out_shape=out_shape,
        scratch_shapes=list(scratch),
        compiler_params=pltpu.CompilerParams(vmem_limit_bytes=vmem << 20),
        cost_estimate=pl.CostEstimate(flops=work, bytes_accessed=work, transcendentals=0),
        name=name,
    )


def pack_kernel(up_ref, weight_ref, *refs):
    out_refs, sems = refs[:-1], refs[-1]
    owned, lat, head = up_ref.shape
    width = weight_ref.shape[1]
    copies = []
    for o in range(owned):
        pairs = [(weight_ref.at[pl.ds(o * head, head), :], out_refs[o].at[:, pl.ds(0, width)])]
        for k in range(lat // head):
            pairs.append(
                (
                    up_ref.at[o, pl.ds(k * head, head), :],
                    out_refs[o].at[:, pl.ds(width + k * head, head)],
                )
            )
        for src, dst in pairs:
            copies.append(pltpu.make_async_copy(src, dst, sems.at[len(copies)]))
    for copy in copies:
        copy.start()
    for copy in copies:
        copy.wait()


def pack(ups, weight):
    owned, lat, head = ups.shape
    shape = jax.ShapeDtypeStruct((head, weight.shape[1] + lat), jnp.bfloat16)
    ups = pltpu.with_memory_space_constraint(ups, pltpu.HBM)
    weight = pltpu.with_memory_space_constraint(weight, pltpu.HBM)
    sems = pltpu.SemaphoreType.DMA((owned * (1 + lat // head),))
    return call(
        pack_kernel, "pack", [shape] * owned, [ANY] * 2, [sems], out_specs=[ANY] * owned, vmem=1
    )(ups, weight)


def load_kernel(cache_ref, query_ref, out_cache_ref, out_query_ref, sems):
    rows = cache_ref.shape[0]
    copies = [pltpu.make_async_copy(query_ref, out_query_ref, sems.at[rows])]
    for row in range(rows):
        copies.append(
            pltpu.make_async_copy(cache_ref.at[row], out_cache_ref.at[row], sems.at[row])
        )
    for copy in copies:
        copy.start()
    for copy in copies:
        copy.wait()


def load(cache, queries):
    rows = cache.shape[0]
    cache = pltpu.with_memory_space_constraint(cache, pltpu.HBM)
    queries = pltpu.with_memory_space_constraint(queries, pltpu.HBM)
    return call(
        load_kernel,
        "load",
        [pltpu.VMEM(cache.shape, cache.dtype), pltpu.VMEM(queries.shape, queries.dtype)],
        [ANY] * 2,
        [pltpu.SemaphoreType.DMA((rows + 1,))],
        out_specs=[VMEM, VMEM],
        vmem=1,
        work=12 << 20,
    )(cache, queries)


def split_logsum(logsum):
    high = logsum.astype(jnp.bfloat16).astype(jnp.float32)
    middle = (logsum - high).astype(jnp.bfloat16).astype(jnp.float32)
    return [high, middle, logsum - high - middle]


def stat_block(logsums, width):
    parts = [part for logsum in logsums for part in split_logsum(logsum)]
    parts.append(jnp.zeros((STAT_ROWS - len(parts), parts[0].shape[1]), jnp.float32))
    block = jnp.concatenate(parts, axis=0)
    return jnp.concatenate([block, jnp.zeros((STAT_ROWS, width - block.shape[1]), jnp.float32)], axis=1)


def attend_kernel(lat, place_ref, length_ref, *refs):
    query_parts, (cache_ref, mine_ref, theirs_ref, query_ref, score_ref, weight_ref) = refs[:-6], refs[-6:]
    rows, block, _ = query_parts[0].shape
    heads = block * len(query_parts)
    span = cache_ref.shape[2]
    context, core = place_ref[0], place_ref[1]
    for k, part in enumerate(query_parts):
        first = pl.multiple_of((context ^ k) * block, block)
        for row in range(rows):
            query_ref[row, pl.ds(first, block), :] = part[row]

    positions = lax.broadcasted_iota(jnp.int32, (1, span), 1) + context * span

    def score(row):
        scores = product(query_ref[row], cache_ref[row], 1, 0)
        scores = jnp.where(positions < length_ref[row], scores, DEAD)
        score_ref[row % 2] = scores
        return jnp.max(scores, axis=1, keepdims=True)

    def weigh(row, peak):
        weights = jnp.exp2((score_ref[row % 2] - peak) * (SCALE * LOG2E))
        weight_ref[row % 2] = weights.astype(jnp.bfloat16)
        return jnp.sum(weights, axis=1, keepdims=True)

    half = lat // 2
    logsums = []

    def mix(row, peak, total):
        mixed = product(weight_ref[row % 2], cache_ref[row, :lat], 1, 1)
        mixed = (mixed / total).astype(jnp.bfloat16).astype(jnp.float32)
        low, high = mixed[:, :half], mixed[:, half:]
        place = slice(row * heads, (row + 1) * heads)
        mine_ref[place, :] = jnp.where(core == 0, low, high).astype(jnp.bfloat16)
        theirs_ref[place, :] = jnp.where(core == 0, high, low).astype(jnp.bfloat16)
        logsum = peak * SCALE + jnp.log(total)
        logsums.append(jnp.broadcast_to(logsum, (heads, heads)).T[0:1])

    peak = score(0)
    for row in range(rows):
        total = weigh(row, peak)
        following = score(row + 1) if row + 1 < rows else None
        mix(row, peak, total)
        peak = following
    stats = stat_block(logsums, half).astype(jnp.bfloat16)
    mine_ref[rows * heads :, :] = stats
    theirs_ref[rows * heads :, :] = stats


def attend(places, lengths, query_parts, cache, lat):
    rows, block, width = query_parts[0].shape
    heads = block * len(query_parts)
    span = cache.shape[2]
    shape = jax.ShapeDtypeStruct((rows * heads + STAT_ROWS, lat // 2), jnp.bfloat16)
    cache = pltpu.with_memory_space_constraint(cache, pltpu.VMEM)
    return call(
        functools.partial(attend_kernel, lat),
        "attend",
        [shape, shape],
        [SMEM, SMEM] + [VMEM] * (len(query_parts) + 1),
        [
            pltpu.VMEM((rows, heads, width), jnp.bfloat16),
            pltpu.VMEM((2, heads, span), jnp.float32),
            pltpu.VMEM((2, heads, span), jnp.bfloat16),
        ],
    )(places, lengths, *query_parts, cache)


def merge_states(rows, heads, refs):
    stats = [ref[rows * heads :, :heads].astype(jnp.float32) for ref in refs]
    shares, merged_logsums = [], []
    for row in range(rows):
        logsums = [sum(s[3 * row + k : 3 * row + k + 1] for k in range(3)) for s in stats]
        peak = functools.reduce(jnp.maximum, logsums)
        factors = [jnp.exp(v - peak) for v in logsums]
        total = functools.reduce(jnp.add, factors)
        shares += [f / total for f in factors]
        merged_logsums.append(peak + jnp.log(total))
    shares.append(jnp.zeros((heads - len(shares), heads), jnp.float32))
    shares = jnp.concatenate(shares, axis=0).T
    merged = []
    for row in range(rows):
        terms = []
        for c, ref in enumerate(refs):
            column = row * len(refs) + c
            values = ref[row * heads : (row + 1) * heads, :].astype(jnp.float32)
            terms.append(shares[:, column : column + 1] * values)
        merged.append(sum(terms).astype(jnp.bfloat16))
    return merged, merged_logsums


def merge_kernel(rows, heads, a_ref, b_ref, out_ref):
    merged, logsums = merge_states(rows, heads, (a_ref, b_ref))
    for row in range(rows):
        out_ref[row * heads : (row + 1) * heads, :] = merged[row]
    out_ref[rows * heads :, :] = stat_block(logsums, out_ref.shape[1]).astype(jnp.bfloat16)


def merge(a, b, rows, heads):
    shape = jax.ShapeDtypeStruct(a.shape, jnp.bfloat16)
    return call(functools.partial(merge_kernel, rows, heads), "merge", shape, [VMEM, VMEM])(a, b)


def finish_kernel(rows, heads, owned, sizes, a_ref, b_ref, out_ref):
    merged, _ = merge_states(rows, heads, (a_ref, b_ref))
    merged = jnp.concatenate(merged, axis=0)
    _, x, yh = sizes
    place = lax.broadcasted_iota(jnp.int32, (rows * heads, 1), 0)
    row, place = place % rows, place // rows
    head, place = place % owned, place // owned
    across, place = place % x, place // x
    side, deep = place % yh, place // yh
    source = row * heads + ((deep * x + across) * yh + side) * owned + head
    columns = lax.broadcasted_iota(jnp.int32, (1, rows * heads), 1)
    order = jnp.where(columns == source, 1.0, 0.0).astype(jnp.bfloat16)
    out_ref[...] = product(order, merged, 1, 0).astype(jnp.bfloat16)


def finish(a, b, rows, heads, owned, sizes):
    shape = jax.ShapeDtypeStruct((rows * heads, a.shape[1]), jnp.bfloat16)
    kernel = functools.partial(finish_kernel, rows, heads, owned, sizes)
    return call(kernel, "finish", shape, [VMEM] * 2)(a, b)


def project_kernel(rows, owned, width, place_ref, mine_ref, theirs_ref, *refs):
    tiles, (out_ref, sorted_ref) = refs[:-2], refs[-2:]
    core, here = place_ref[1], place_ref[2]
    half = mine_ref.shape[1]
    peers = out_ref.shape[0]
    count = mine_ref.shape[0] // (peers * rows)
    target = lax.broadcasted_iota(jnp.int32, (sorted_ref.shape[0], 1), 0)
    slot, target = target % SLOTS, target // SLOTS
    holder, group = target % peers, target // peers
    source = jnp.where(slot < rows, (holder * count + group) * rows + slot, -1)
    columns = lax.broadcasted_iota(jnp.int32, (1, mine_ref.shape[0]), 1)
    select = jnp.where(columns == source, 1.0, 0.0).astype(jnp.bfloat16)
    mine = product(select, mine_ref[...], 1, 0).astype(jnp.bfloat16)
    theirs = product(select, theirs_ref[...], 1, 0).astype(jnp.bfloat16)
    sorted_ref[:, :half] = jnp.where(core == 0, mine, theirs)
    sorted_ref[:, half:] = jnp.where(core == 0, theirs, mine)
    slots = peers * SLOTS
    ring = count // owned
    result = None
    for k, distance in enumerate((0, ring - 1, 1, 2)):
        pieces = tiles[k * owned : (k + 1) * owned]
        heads_out = []
        for o, tile in enumerate(pieces):
            head = tile.shape[0]
            first = ((here + distance) % ring * owned + o) * slots
            lines = sorted_ref[pl.ds(pl.multiple_of(first, slots), slots), :]
            up = [tile[:, width + j * head : width + (j + 1) * head] for j in range(2 * half // head)]
            up = jnp.concatenate(up, axis=0)
            heads_out.append(product(lines, up, 1, 0).astype(jnp.bfloat16))
        weight = jnp.concatenate([tile[:, :width] for tile in pieces], axis=0)
        term = product(jnp.concatenate(heads_out, axis=1), weight, 1, 0)
        result = term if result is None else result + term
    result = result.astype(jnp.bfloat16)
    for d in range(peers):
        out_ref[d] = result[d * SLOTS : d * SLOTS + rows, :]


def project(places, mine, theirs, tiles, peers, rows, owned, width):
    ring = mine.shape[0] // (peers * rows * owned)
    lines = ring * owned * peers * SLOTS
    return call(
        functools.partial(project_kernel, rows, owned, width),
        "project",
        jax.ShapeDtypeStruct((peers, rows, width), jnp.bfloat16),
        [SMEM] + [VMEM] * (2 + len(tiles)),
        [pltpu.VMEM((lines, 2 * mine.shape[1]), jnp.bfloat16)],
    )(places, mine, theirs, *tiles)


def from_x(block, distance):
    size = lax.axis_size("x")
    return lax.ppermute(block, "x", [(i, (i + distance) % size) for i in range(size)])


def shards(queries, cache, lengths, ups, weight):
    rows = queries.shape[0]
    owned, lat, _ = ups.shape
    sizes = tuple(lax.axis_size(a) for a in DP)
    heads = math.prod(sizes) * owned
    peers = math.prod(lax.axis_size(a) for a in PEERS)
    places = jnp.stack([lax.axis_index(CTX), lax.axis_index("core"), lax.axis_index("x")])

    across = swap(queries, "yl")
    partner = swap(queries, "core")
    own = pack(ups, weight)
    behind, ahead = from_x(own[0], 1), from_x(own[1], -1)

    cache, held = load(jnp.swapaxes(cache, 1, 2), queries)
    query_parts = [held, partner, across, swap(across, "core")]
    mine, theirs = attend(places, lengths, query_parts, cache, lat)
    state = merge(mine, swap(theirs, "core"), rows, heads)
    state, behind, ahead, own = lax.optimization_barrier((state, behind, ahead, own))
    tiles = [
        *own,
        *(behind, from_x(own[1], 1)),
        *(from_x(own[0], -1), ahead),
        *(from_x(behind, 1), from_x(ahead, -1)),
    ]
    latents = finish(state, swap(state, "yl"), rows, heads, owned, sizes)

    latents = latents.reshape(peers, -1, lat // 2)
    latents = lax.all_to_all(latents, PEERS, 0, 0, tiled=True)
    latents = latents.reshape(rows * heads, lat // 2)
    partial = project(
        places, latents, swap(latents, "core"), tiles, peers, rows, owned, weight.shape[1]
    )
    partial = lax.all_to_all(partial, PEERS, 0, 0, tiled=True)
    return jnp.sum(partial.astype(jnp.float32), axis=0).astype(jnp.bfloat16)


def solution(mesh):
    inner = Mesh(mesh.devices.reshape(8, 4, 2, 2, 2), DP + CTX)
    return jax.shard_map(
        shards,
        mesh=inner,
        in_specs=(
            P(DP, CTX, None),
            P(DP, CTX, None),
            P(DP),
            P(DP, None, None),
            P(DP, CTX),
        ),
        out_specs=P(DP, CTX),
        check_vma=False,
    )
```

```python
import functools
import math

import jax
import jax.numpy as jnp
import numpy as np
from jax import lax
from jax.experimental import pallas as pl
from jax.experimental.pallas import tpu as pltpu
from jax.sharding import Mesh, PartitionSpec as P

ROPE = 64
QK = 128
SCALE = (QK + ROPE) ** -0.5
LOG2E = math.log2(math.e)
DEAD = -1e30
DP = ("z", "x", "yh")
PEERS = ("z", "yh")
CTX = ("yl", "core")
STAT_ROWS = 16
SLOTS = 4
VMEM = pl.BlockSpec(memory_space=pltpu.VMEM)
SMEM = pl.BlockSpec(memory_space=pltpu.SMEM)
ANY = pl.BlockSpec(memory_space=pl.ANY)


def product(a, b, dim_a, dim_b):
    return lax.dot_general(
        a, b, (((dim_a,), (dim_b,)), ((), ())), preferred_element_type=jnp.float32
    )


def swap(block, axis):
    return lax.ppermute(block, axis, [(0, 1), (1, 0)])


def call(kernel, name, out_shape, in_specs, scratch=(), out_specs=None, vmem=24, work=0):
    return pl.pallas_call(
        kernel,
        in_specs=in_specs,
        out_specs=jax.tree.map(lambda _: VMEM, out_shape) if out_specs is None else out_specs,
        out_shape=out_shape,
        scratch_shapes=list(scratch),
        compiler_params=pltpu.CompilerParams(vmem_limit_bytes=vmem << 20),
        cost_estimate=pl.CostEstimate(flops=work, bytes_accessed=work, transcendentals=0),
        name=name,
    )


def pack_kernel(up_ref, weight_ref, *refs):
    out_refs, sems = refs[:-1], refs[-1]
    owned, lat, head = up_ref.shape
    width = weight_ref.shape[1]
    copies = []
    for o in range(owned):
        pairs = [(weight_ref.at[pl.ds(o * head, head), :], out_refs[o].at[:, pl.ds(0, width)])]
        for k in range(lat // head):
            pairs.append(
                (
                    up_ref.at[o, pl.ds(k * head, head), :],
                    out_refs[o].at[:, pl.ds(width + k * head, head)],
                )
            )
        for src, dst in pairs:
            copies.append(pltpu.make_async_copy(src, dst, sems.at[len(copies)]))
    for copy in copies:
        copy.start()
    for copy in copies:
        copy.wait()


def pack(ups, weight):
    owned, lat, head = ups.shape
    shape = jax.ShapeDtypeStruct((head, weight.shape[1] + lat), jnp.bfloat16)
    ups = pltpu.with_memory_space_constraint(ups, pltpu.HBM)
    weight = pltpu.with_memory_space_constraint(weight, pltpu.HBM)
    sems = pltpu.SemaphoreType.DMA((owned * (1 + lat // head),))
    return call(
        pack_kernel, "pack", [shape] * owned, [ANY] * 2, [sems], out_specs=[ANY] * owned, vmem=1
    )(ups, weight)


def load_kernel(cache_ref, query_ref, out_cache_ref, out_query_ref, sems):
    rows = cache_ref.shape[0]
    copies = [pltpu.make_async_copy(query_ref, out_query_ref, sems.at[rows])]
    for row in range(rows):
        copies.append(
            pltpu.make_async_copy(cache_ref.at[row], out_cache_ref.at[row], sems.at[row])
        )
    for copy in copies:
        copy.start()
    for copy in copies:
        copy.wait()


def load(cache, queries):
    rows = cache.shape[0]
    cache = pltpu.with_memory_space_constraint(cache, pltpu.HBM)
    queries = pltpu.with_memory_space_constraint(queries, pltpu.HBM)
    return call(
        load_kernel,
        "load",
        [pltpu.VMEM(cache.shape, cache.dtype), pltpu.VMEM(queries.shape, queries.dtype)],
        [ANY] * 2,
        [pltpu.SemaphoreType.DMA((rows + 1,))],
        out_specs=[VMEM, VMEM],
        vmem=1,
        work=12 << 20,
    )(cache, queries)


def split_logsum(logsum):
    high = logsum.astype(jnp.bfloat16).astype(jnp.float32)
    middle = (logsum - high).astype(jnp.bfloat16).astype(jnp.float32)
    return [high, middle, logsum - high - middle]


def stat_block(logsums, width):
    parts = [part for logsum in logsums for part in split_logsum(logsum)]
    parts.append(jnp.zeros((STAT_ROWS - len(parts), parts[0].shape[1]), jnp.float32))
    block = jnp.concatenate(parts, axis=0)
    return jnp.concatenate([block, jnp.zeros((STAT_ROWS, width - block.shape[1]), jnp.float32)], axis=1)


def attend_kernel(lat, place_ref, length_ref, *refs):
    query_parts, (cache_ref, mine_ref, theirs_ref, query_ref, score_ref, weight_ref) = refs[:-6], refs[-6:]
    rows, block, _ = query_parts[0].shape
    heads = block * len(query_parts)
    span = cache_ref.shape[2]
    context, core = place_ref[0], place_ref[1]
    for k, part in enumerate(query_parts):
        first = pl.multiple_of((context ^ k) * block, block)
        for row in range(rows):
            query_ref[row, pl.ds(first, block), :] = part[row]

    positions = lax.broadcasted_iota(jnp.int32, (1, span), 1) + context * span

    def score(row):
        scores = product(query_ref[row], cache_ref[row], 1, 0)
        scores = jnp.where(positions < length_ref[row], scores, DEAD)
        score_ref[row % 2] = scores
        return jnp.max(scores, axis=1, keepdims=True)

    def weigh(row, peak):
        weights = jnp.exp2((score_ref[row % 2] - peak) * (SCALE * LOG2E))
        weight_ref[row % 2] = weights.astype(jnp.bfloat16)
        return jnp.sum(weights, axis=1, keepdims=True)

    half = lat // 2
    logsums = []

    def mix(row, peak, total):
        mixed = product(weight_ref[row % 2], cache_ref[row, :lat], 1, 1)
        mixed = (mixed / total).astype(jnp.bfloat16).astype(jnp.float32)
        low, high = mixed[:, :half], mixed[:, half:]
        place = slice(row * heads, (row + 1) * heads)
        mine_ref[place, :] = jnp.where(core == 0, low, high).astype(jnp.bfloat16)
        theirs_ref[place, :] = jnp.where(core == 0, high, low).astype(jnp.bfloat16)
        logsum = peak * SCALE + jnp.log(total)
        logsums.append(jnp.broadcast_to(logsum, (heads, heads)).T[0:1])

    peak = score(0)
    for row in range(rows):
        total = weigh(row, peak)
        following = score(row + 1) if row + 1 < rows else None
        mix(row, peak, total)
        peak = following
    stats = stat_block(logsums, half).astype(jnp.bfloat16)
    mine_ref[rows * heads :, :] = stats
    theirs_ref[rows * heads :, :] = stats


def attend(places, lengths, query_parts, cache, lat):
    rows, block, width = query_parts[0].shape
    heads = block * len(query_parts)
    span = cache.shape[2]
    shape = jax.ShapeDtypeStruct((rows * heads + STAT_ROWS, lat // 2), jnp.bfloat16)
    cache = pltpu.with_memory_space_constraint(cache, pltpu.VMEM)
    return call(
        functools.partial(attend_kernel, lat),
        "attend",
        [shape, shape],
        [SMEM, SMEM] + [VMEM] * (len(query_parts) + 1),
        [
            pltpu.VMEM((rows, heads, width), jnp.bfloat16),
            pltpu.VMEM((2, heads, span), jnp.float32),
            pltpu.VMEM((2, heads, span), jnp.bfloat16),
        ],
    )(places, lengths, *query_parts, cache)


def merge_states(rows, heads, refs):
    stats = [ref[rows * heads :, :heads].astype(jnp.float32) for ref in refs]
    shares, merged_logsums = [], []
    for row in range(rows):
        logsums = [sum(s[3 * row + k : 3 * row + k + 1] for k in range(3)) for s in stats]
        peak = functools.reduce(jnp.maximum, logsums)
        factors = [jnp.exp(v - peak) for v in logsums]
        total = functools.reduce(jnp.add, factors)
        shares += [f / total for f in factors]
        merged_logsums.append(peak + jnp.log(total))
    shares.append(jnp.zeros((heads - len(shares), heads), jnp.float32))
    shares = jnp.concatenate(shares, axis=0).T
    merged = []
    for row in range(rows):
        terms = []
        for c, ref in enumerate(refs):
            column = row * len(refs) + c
            values = ref[row * heads : (row + 1) * heads, :].astype(jnp.float32)
            terms.append(shares[:, column : column + 1] * values)
        merged.append(sum(terms).astype(jnp.bfloat16))
    return merged, merged_logsums


def merge_kernel(rows, heads, a_ref, b_ref, out_ref):
    merged, logsums = merge_states(rows, heads, (a_ref, b_ref))
    for row in range(rows):
        out_ref[row * heads : (row + 1) * heads, :] = merged[row]
    out_ref[rows * heads :, :] = stat_block(logsums, out_ref.shape[1]).astype(jnp.bfloat16)


def merge(a, b, rows, heads):
    shape = jax.ShapeDtypeStruct(a.shape, jnp.bfloat16)
    return call(functools.partial(merge_kernel, rows, heads), "merge", shape, [VMEM, VMEM])(a, b)


def finish_kernel(rows, heads, owned, sizes, a_ref, b_ref, out_ref):
    merged, _ = merge_states(rows, heads, (a_ref, b_ref))
    merged = jnp.concatenate(merged, axis=0)
    _, x, yh = sizes
    column = lax.broadcasted_iota(jnp.int32, (1, rows * heads), 1)
    row, head = column // heads, column % heads
    own, head = head % owned, head // owned
    side, head = head % yh, head // yh
    across, deep = head % x, head // x
    target = (((deep * yh + side) * x + across) * owned + own) * rows + row
    lines = lax.broadcasted_iota(jnp.int32, (rows * heads, 1), 0)
    order = jnp.where(lines == target, 1.0, 0.0).astype(jnp.bfloat16)
    out_ref[...] = product(order, merged, 1, 0).astype(jnp.bfloat16)


def finish(a, b, rows, heads, owned, sizes):
    shape = jax.ShapeDtypeStruct((rows * heads, a.shape[1]), jnp.bfloat16)
    kernel = functools.partial(finish_kernel, rows, heads, owned, sizes)
    return call(kernel, "finish", shape, [VMEM] * 2)(a, b)


def project_lines(lines, pieces, width):
    heads_out = []
    for rows, tile in zip(lines, pieces):
        head = tile.shape[0]
        up = [tile[:, j : j + head] for j in range(width, tile.shape[1], head)]
        heads_out.append(product(rows, jnp.concatenate(up, axis=0), 1, 0).astype(jnp.bfloat16))
    weight = jnp.concatenate([tile[:, :width] for tile in pieces], axis=0)
    return product(jnp.concatenate(heads_out, axis=1), weight, 1, 0)


def near_kernel(rows, owned, width, place_ref, mine_ref, theirs_ref, *refs):
    tiles, (sum_ref, far_ref, sorted_ref) = refs[:-3], refs[-3:]
    core, here = place_ref[1], place_ref[2]
    half = mine_ref.shape[1]
    slots = sum_ref.shape[0]
    peers = slots // SLOTS
    count = mine_ref.shape[0] // (peers * rows)
    target = lax.broadcasted_iota(jnp.int32, (sorted_ref.shape[0], 1), 0)
    slot, target = target % SLOTS, target // SLOTS
    holder, group = target % peers, target // peers
    source = jnp.where(slot < rows, (holder * count + group) * rows + slot, -1)
    columns = lax.broadcasted_iota(jnp.int32, (1, mine_ref.shape[0]), 1)
    select = jnp.where(columns == source, 1.0, 0.0).astype(jnp.bfloat16)
    mine, theirs = mine_ref[...], theirs_ref[...]
    low, high = jnp.where(core == 0, mine, theirs), jnp.where(core == 0, theirs, mine)
    sorted_ref[:, :half] = product(select, low, 1, 0).astype(jnp.bfloat16)
    sorted_ref[:, half:] = product(select, high, 1, 0).astype(jnp.bfloat16)
    ring = count // owned

    def lines(distance, o):
        first = ((here + distance) % ring * owned + o) * slots
        return sorted_ref[pl.ds(pl.multiple_of(first, slots), slots), :]

    result = None
    for k, distance in enumerate((0, ring - 1, 1)):
        pieces = tiles[k * owned : (k + 1) * owned]
        term = project_lines([lines(distance, o) for o in range(owned)], pieces, width)
        result = term if result is None else result + term
    sum_ref[...] = result
    for o in range(owned):
        far_ref[o * slots : (o + 1) * slots, :] = lines(2, o)


def project_near(places, mine, theirs, tiles, peers, rows, owned, width):
    count = mine.shape[0] // (peers * rows)
    slots = peers * SLOTS
    lat = 2 * mine.shape[1]
    return call(
        functools.partial(near_kernel, rows, owned, width),
        "project_near",
        [
            jax.ShapeDtypeStruct((slots, width), jnp.float32),
            jax.ShapeDtypeStruct((owned * slots, lat), jnp.bfloat16),
        ],
        [SMEM] + [VMEM] * (2 + len(tiles)),
        [pltpu.VMEM((count * slots, lat), jnp.bfloat16)],
    )(places, mine, theirs, *tiles)


def far_kernel(rows, width, sum_ref, line_ref, *refs):
    tiles, out_ref = refs[:-1], refs[-1]
    slots = sum_ref.shape[0]
    lines = [line_ref[o * slots : (o + 1) * slots, :] for o in range(len(tiles))]
    result = (sum_ref[...] + project_lines(lines, tiles, width)).astype(jnp.bfloat16)
    for d in range(out_ref.shape[0]):
        out_ref[d] = result[d * SLOTS : d * SLOTS + rows, :]


def project_far(near, lines, tiles, peers, rows, width):
    return call(
        functools.partial(far_kernel, rows, width),
        "project_far",
        jax.ShapeDtypeStruct((peers, rows, width), jnp.bfloat16),
        [VMEM] * (2 + len(tiles)),
    )(near, lines, *tiles)


def from_x(block, distance):
    size = lax.axis_size("x")
    return lax.ppermute(block, "x", [(i, (i + distance) % size) for i in range(size)])


def shards(queries, cache, lengths, ups, weight):
    rows = queries.shape[0]
    owned, lat, _ = ups.shape
    sizes = tuple(lax.axis_size(a) for a in DP)
    heads = math.prod(sizes) * owned
    peers = math.prod(lax.axis_size(a) for a in PEERS)
    places = jnp.stack([lax.axis_index(CTX), lax.axis_index("core"), lax.axis_index("x")])

    across = swap(queries, "yl")
    partner = swap(queries, "core")
    own = pack(ups, weight)
    behind, ahead = from_x(own[0], 1), from_x(own[1], -1)

    cache, held = load(jnp.swapaxes(cache, 1, 2), queries)
    query_parts = [held, partner, across, swap(across, "core")]
    mine, theirs = attend(places, lengths, query_parts, cache, lat)
    theirs, own = lax.optimization_barrier((theirs, own))
    behind_too, ahead_too = from_x(own[1], 1), from_x(own[0], -1)
    state = merge(mine, swap(theirs, "core"), rows, heads)
    state, behind, ahead = lax.optimization_barrier((state, behind, ahead))
    tiles = [*own, behind, behind_too, ahead_too, ahead, from_x(behind, 1), from_x(ahead, -1)]
    latents = finish(state, swap(state, "yl"), rows, heads, owned, sizes)

    latents = latents.reshape(peers, -1, lat // 2)
    latents = lax.all_to_all(latents, PEERS, 0, 0, tiled=True)
    latents = latents.reshape(rows * heads, lat // 2)
    width = weight.shape[1]
    theirs = swap(latents, "core")
    near, lines = project_near(places, latents, theirs, tiles[:-2], peers, rows, owned, width)
    partial = project_far(near, lines, tiles[-2:], peers, rows, width)
    partial = lax.all_to_all(partial, PEERS, 0, 0, tiled=True)
    return jnp.sum(partial.astype(jnp.float32), axis=0).astype(jnp.bfloat16)


def solution(mesh):
    inner = Mesh(mesh.devices.reshape(8, 4, 2, 2, 2), DP + CTX)
    return jax.shard_map(
        shards,
        mesh=inner,
        in_specs=(
            P(DP, CTX, None),
            P(DP, CTX, None),
            P(DP),
            P(DP, None, None),
            P(DP, CTX),
        ),
        out_specs=P(DP, CTX),
        check_vma=False,
    )
```

```python
import functools
import math

import jax
import jax.numpy as jnp
import numpy as np
from jax import lax
from jax.experimental import pallas as pl
from jax.experimental.pallas import tpu as pltpu
from jax.sharding import Mesh, PartitionSpec as P

ROPE = 64
QK = 128
SCALE = (QK + ROPE) ** -0.5
LOG2E = math.log2(math.e)
DEAD = -1e30
DP = ("z", "x", "yh")
PEERS = ("z", "yh")
CTX = ("yl", "core")
STAT_ROWS = 16
SLOTS = 4
VMEM = pl.BlockSpec(memory_space=pltpu.VMEM)
SMEM = pl.BlockSpec(memory_space=pltpu.SMEM)
ANY = pl.BlockSpec(memory_space=pl.ANY)


def product(a, b, dim_a, dim_b):
    return lax.dot_general(
        a, b, (((dim_a,), (dim_b,)), ((), ())), preferred_element_type=jnp.float32
    )


def swap(block, axis):
    return lax.ppermute(block, axis, [(0, 1), (1, 0)])


def call(kernel, name, out_shape, in_specs, scratch=(), out_specs=None, vmem=24, work=0):
    return pl.pallas_call(
        kernel,
        in_specs=in_specs,
        out_specs=jax.tree.map(lambda _: VMEM, out_shape) if out_specs is None else out_specs,
        out_shape=out_shape,
        scratch_shapes=list(scratch),
        compiler_params=pltpu.CompilerParams(vmem_limit_bytes=vmem << 20),
        cost_estimate=pl.CostEstimate(flops=work, bytes_accessed=work, transcendentals=0),
        name=name,
    )


def pack_kernel(up_ref, weight_ref, *refs):
    out_refs, sems = refs[:-1], refs[-1]
    owned, lat, head = up_ref.shape
    width = weight_ref.shape[1]
    copies = []
    for o in range(owned):
        pairs = [(weight_ref.at[pl.ds(o * head, head), :], out_refs[o].at[:, pl.ds(0, width)])]
        for k in range(lat // head):
            pairs.append(
                (
                    up_ref.at[o, pl.ds(k * head, head), :],
                    out_refs[o].at[:, pl.ds(width + k * head, head)],
                )
            )
        for src, dst in pairs:
            copies.append(pltpu.make_async_copy(src, dst, sems.at[len(copies)]))
    for copy in copies:
        copy.start()
    for copy in copies:
        copy.wait()


def pack(ups, weight):
    owned, lat, head = ups.shape
    shape = jax.ShapeDtypeStruct((head, weight.shape[1] + lat), jnp.bfloat16)
    ups = pltpu.with_memory_space_constraint(ups, pltpu.HBM)
    weight = pltpu.with_memory_space_constraint(weight, pltpu.HBM)
    sems = pltpu.SemaphoreType.DMA((owned * (1 + lat // head),))
    return call(
        pack_kernel, "pack", [shape] * owned, [ANY] * 2, [sems], out_specs=[ANY] * owned, vmem=1
    )(ups, weight)


def load_kernel(cache_ref, query_ref, out_cache_ref, out_query_ref, sems):
    rows = cache_ref.shape[0]
    copies = [pltpu.make_async_copy(query_ref, out_query_ref, sems.at[rows])]
    for row in range(rows):
        copies.append(
            pltpu.make_async_copy(cache_ref.at[row], out_cache_ref.at[row], sems.at[row])
        )
    for copy in copies:
        copy.start()
    for copy in copies:
        copy.wait()


def load(cache, queries):
    rows = cache.shape[0]
    cache = pltpu.with_memory_space_constraint(cache, pltpu.HBM)
    queries = pltpu.with_memory_space_constraint(queries, pltpu.HBM)
    return call(
        load_kernel,
        "load",
        [pltpu.VMEM(cache.shape, cache.dtype), pltpu.VMEM(queries.shape, queries.dtype)],
        [ANY] * 2,
        [pltpu.SemaphoreType.DMA((rows + 1,))],
        out_specs=[VMEM, VMEM],
        vmem=1,
        work=12 << 20,
    )(cache, queries)


def split_logsum(logsum):
    high = logsum.astype(jnp.bfloat16).astype(jnp.float32)
    middle = (logsum - high).astype(jnp.bfloat16).astype(jnp.float32)
    return [high, middle, logsum - high - middle]


def stat_block(logsums, width):
    parts = [part for logsum in logsums for part in split_logsum(logsum)]
    parts.append(jnp.zeros((STAT_ROWS - len(parts), parts[0].shape[1]), jnp.float32))
    block = jnp.concatenate(parts, axis=0)
    return jnp.concatenate([block, jnp.zeros((STAT_ROWS, width - block.shape[1]), jnp.float32)], axis=1)


def attend_kernel(lat, place_ref, length_ref, *refs):
    query_parts, (cache_ref, mine_ref, theirs_ref, query_ref, score_ref, weight_ref) = refs[:-6], refs[-6:]
    rows, block, _ = query_parts[0].shape
    heads = block * len(query_parts)
    span = cache_ref.shape[2]
    context, core = place_ref[0], place_ref[1]
    for k, part in enumerate(query_parts):
        first = pl.multiple_of((context ^ k) * block, block)
        for row in range(rows):
            query_ref[row, pl.ds(first, block), :] = part[row]

    positions = lax.broadcasted_iota(jnp.int32, (1, span), 1) + context * span

    def score(row):
        scores = product(query_ref[row], cache_ref[row], 1, 0)
        scores = jnp.where(positions < length_ref[row], scores, DEAD)
        score_ref[row % 2] = scores
        return jnp.max(scores, axis=1, keepdims=True)

    def weigh(row, peak):
        weights = jnp.exp2((score_ref[row % 2] - peak) * (SCALE * LOG2E))
        weight_ref[row % 2] = weights.astype(jnp.bfloat16)
        return jnp.sum(weights, axis=1, keepdims=True)

    half = lat // 2
    logsums = []

    def mix(row, peak, total):
        mixed = product(weight_ref[row % 2], cache_ref[row, :lat], 1, 1)
        mixed = (mixed / total).astype(jnp.bfloat16).astype(jnp.float32)
        low, high = mixed[:, :half], mixed[:, half:]
        place = slice(row * heads, (row + 1) * heads)
        mine_ref[place, :] = jnp.where(core == 0, low, high).astype(jnp.bfloat16)
        theirs_ref[place, :] = jnp.where(core == 0, high, low).astype(jnp.bfloat16)
        logsum = peak * SCALE + jnp.log(total)
        logsums.append(jnp.broadcast_to(logsum, (heads, heads)).T[0:1])

    peak = score(0)
    for row in range(rows):
        total = weigh(row, peak)
        following = score(row + 1) if row + 1 < rows else None
        mix(row, peak, total)
        peak = following
    stats = stat_block(logsums, half).astype(jnp.bfloat16)
    mine_ref[rows * heads :, :] = stats
    theirs_ref[rows * heads :, :] = stats


def attend(places, lengths, query_parts, cache, lat):
    rows, block, width = query_parts[0].shape
    heads = block * len(query_parts)
    span = cache.shape[2]
    shape = jax.ShapeDtypeStruct((rows * heads + STAT_ROWS, lat // 2), jnp.bfloat16)
    cache = pltpu.with_memory_space_constraint(cache, pltpu.VMEM)
    return call(
        functools.partial(attend_kernel, lat),
        "attend",
        [shape, shape],
        [SMEM, SMEM] + [VMEM] * (len(query_parts) + 1),
        [
            pltpu.VMEM((rows, heads, width), jnp.bfloat16),
            pltpu.VMEM((2, heads, span), jnp.float32),
            pltpu.VMEM((2, heads, span), jnp.bfloat16),
        ],
    )(places, lengths, *query_parts, cache)


def merge_states(rows, heads, refs):
    stats = [ref[rows * heads :, :heads].astype(jnp.float32) for ref in refs]
    shares, merged_logsums = [], []
    for row in range(rows):
        logsums = [sum(s[3 * row + k : 3 * row + k + 1] for k in range(3)) for s in stats]
        peak = functools.reduce(jnp.maximum, logsums)
        factors = [jnp.exp(v - peak) for v in logsums]
        total = functools.reduce(jnp.add, factors)
        shares += [f / total for f in factors]
        merged_logsums.append(peak + jnp.log(total))
    shares.append(jnp.zeros((heads - len(shares), heads), jnp.float32))
    shares = jnp.concatenate(shares, axis=0).T
    merged = []
    for row in range(rows):
        terms = []
        for c, ref in enumerate(refs):
            column = row * len(refs) + c
            values = ref[row * heads : (row + 1) * heads, :].astype(jnp.float32)
            terms.append(shares[:, column : column + 1] * values)
        merged.append(sum(terms).astype(jnp.bfloat16))
    return merged, merged_logsums


def merge_kernel(rows, heads, a_ref, b_ref, out_ref):
    merged, logsums = merge_states(rows, heads, (a_ref, b_ref))
    for row in range(rows):
        out_ref[row * heads : (row + 1) * heads, :] = merged[row]
    out_ref[rows * heads :, :] = stat_block(logsums, out_ref.shape[1]).astype(jnp.bfloat16)


def merge(a, b, rows, heads):
    shape = jax.ShapeDtypeStruct(a.shape, jnp.bfloat16)
    return call(functools.partial(merge_kernel, rows, heads), "merge", shape, [VMEM, VMEM])(a, b)


def finish_kernel(rows, heads, owned, sizes, a_ref, b_ref, out_ref):
    merged, _ = merge_states(rows, heads, (a_ref, b_ref))
    merged = jnp.concatenate(merged, axis=0)
    _, x, yh = sizes
    column = lax.broadcasted_iota(jnp.int32, (1, rows * heads), 1)
    row, head = column // heads, column % heads
    own, head = head % owned, head // owned
    side, head = head % yh, head // yh
    across, deep = head % x, head // x
    target = (((deep * yh + side) * x + across) * owned + own) * rows + row
    lines = lax.broadcasted_iota(jnp.int32, (rows * heads, 1), 0)
    order = jnp.where(lines == target, 1.0, 0.0).astype(jnp.bfloat16)
    out_ref[...] = product(order, merged, 1, 0).astype(jnp.bfloat16)


def finish(a, b, rows, heads, owned, sizes):
    shape = jax.ShapeDtypeStruct((rows * heads, a.shape[1]), jnp.bfloat16)
    kernel = functools.partial(finish_kernel, rows, heads, owned, sizes)
    return call(kernel, "finish", shape, [VMEM] * 2)(a, b)


def project_lines(lines, pieces, width):
    heads_out = []
    for rows, tile in zip(lines, pieces):
        head = tile.shape[0]
        up = [tile[:, j : j + head] for j in range(width, tile.shape[1], head)]
        heads_out.append(product(rows, jnp.concatenate(up, axis=0), 1, 0).astype(jnp.bfloat16))
    weight = jnp.concatenate([tile[:, :width] for tile in pieces], axis=0)
    return product(jnp.concatenate(heads_out, axis=1), weight, 1, 0)


def near_kernel(rows, owned, width, place_ref, mine_ref, theirs_ref, *refs):
    tiles, (sum_ref, far_ref, sorted_ref) = refs[:-3], refs[-3:]
    core, here = place_ref[1], place_ref[2]
    half = mine_ref.shape[1]
    slots = sum_ref.shape[0]
    peers = slots // SLOTS
    count = mine_ref.shape[0] // (peers * rows)
    target = lax.broadcasted_iota(jnp.int32, (sorted_ref.shape[0], 1), 0)
    slot, target = target % SLOTS, target // SLOTS
    holder, group = target % peers, target // peers
    source = jnp.where(slot < rows, (holder * count + group) * rows + slot, -1)
    columns = lax.broadcasted_iota(jnp.int32, (1, mine_ref.shape[0]), 1)
    select = jnp.where(columns == source, 1.0, 0.0).astype(jnp.bfloat16)
    mine, theirs = mine_ref[...], theirs_ref[...]
    low, high = jnp.where(core == 0, mine, theirs), jnp.where(core == 0, theirs, mine)
    sorted_ref[:, :half] = product(select, low, 1, 0).astype(jnp.bfloat16)
    sorted_ref[:, half:] = product(select, high, 1, 0).astype(jnp.bfloat16)
    ring = count // owned

    def lines(distance, o):
        first = ((here + distance) % ring * owned + o) * slots
        return sorted_ref[pl.ds(pl.multiple_of(first, slots), slots), :]

    result = None
    for k, distance in enumerate((0, ring - 1, 1)):
        pieces = tiles[k * owned : (k + 1) * owned]
        term = project_lines([lines(distance, o) for o in range(owned)], pieces, width)
        result = term if result is None else result + term
    sum_ref[...] = result
    for o in range(owned):
        far_ref[o * slots : (o + 1) * slots, :] = lines(2, o)


def project_near(places, mine, theirs, tiles, peers, rows, owned, width):
    count = mine.shape[0] // (peers * rows)
    slots = peers * SLOTS
    lat = 2 * mine.shape[1]
    return call(
        functools.partial(near_kernel, rows, owned, width),
        "project_near",
        [
            jax.ShapeDtypeStruct((slots, width), jnp.float32),
            jax.ShapeDtypeStruct((owned * slots, lat), jnp.bfloat16),
        ],
        [SMEM] + [VMEM] * (2 + len(tiles)),
        [pltpu.VMEM((count * slots, lat), jnp.bfloat16)],
    )(places, mine, theirs, *tiles)


def far_kernel(rows, width, sum_ref, line_ref, *refs):
    tiles, out_ref = refs[:-1], refs[-1]
    slots = sum_ref.shape[0]
    lines = [line_ref[o * slots : (o + 1) * slots, :] for o in range(len(tiles))]
    result = (sum_ref[...] + project_lines(lines, tiles, width)).astype(jnp.bfloat16)
    for d in range(out_ref.shape[0]):
        out_ref[d] = result[d * SLOTS : d * SLOTS + rows, :]


def project_far(near, lines, tiles, peers, rows, width):
    return call(
        functools.partial(far_kernel, rows, width),
        "project_far",
        jax.ShapeDtypeStruct((peers, rows, width), jnp.bfloat16),
        [VMEM] * (2 + len(tiles)),
    )(near, lines, *tiles)


def total_kernel(part_ref, out_ref):
    parts = [part_ref[k].astype(jnp.float32) for k in range(part_ref.shape[0])]
    while len(parts) > 1:
        parts = [a + b for a, b in zip(parts[::2], parts[1::2])]
    out_ref[...] = parts[0].astype(jnp.bfloat16)


def total(parts):
    shape = jax.ShapeDtypeStruct(parts.shape[1:], jnp.bfloat16)
    return call(total_kernel, "total", shape, [VMEM])(parts)


def from_x(block, distance):
    size = lax.axis_size("x")
    return lax.ppermute(block, "x", [(i, (i + distance) % size) for i in range(size)])


def shards(queries, cache, lengths, ups, weight):
    rows = queries.shape[0]
    owned, lat, _ = ups.shape
    sizes = tuple(lax.axis_size(a) for a in DP)
    heads = math.prod(sizes) * owned
    peers = math.prod(lax.axis_size(a) for a in PEERS)
    places = jnp.stack([lax.axis_index(CTX), lax.axis_index("core"), lax.axis_index("x")])

    across = swap(queries, "yl")
    partner = swap(queries, "core")
    own = pack(ups, weight)
    behind, ahead = from_x(own[0], 1), from_x(own[1], -1)

    cache, held = load(jnp.swapaxes(cache, 1, 2), queries)
    query_parts = [held, partner, across, swap(across, "core")]
    mine, theirs = attend(places, lengths, query_parts, cache, lat)
    behind_too, ahead_too = from_x(own[1], 1), from_x(own[0], -1)
    state = merge(mine, swap(theirs, "core"), rows, heads)
    state, behind, ahead = lax.optimization_barrier((state, behind, ahead))
    tiles = [*own, behind, behind_too, ahead_too, ahead, from_x(behind, 1), from_x(ahead, -1)]
    latents = finish(state, swap(state, "yl"), rows, heads, owned, sizes)

    latents = latents.reshape(peers, -1, lat // 2)
    latents = lax.all_to_all(latents, PEERS, 0, 0, tiled=True)
    latents = latents.reshape(rows * heads, lat // 2)
    width = weight.shape[1]
    theirs = swap(latents, "core")
    near, lines = project_near(places, latents, theirs, tiles[:-2], peers, rows, owned, width)
    partial = project_far(near, lines, tiles[-2:], peers, rows, width)
    partial = lax.all_to_all(partial, PEERS, 0, 0, tiled=True)
    return total(partial)


def solution(mesh):
    inner = Mesh(mesh.devices.reshape(8, 4, 2, 2, 2), DP + CTX)
    return jax.shard_map(
        shards,
        mesh=inner,
        in_specs=(
            P(DP, CTX, None),
            P(DP, CTX, None),
            P(DP),
            P(DP, None, None),
            P(DP, CTX),
        ),
        out_specs=P(DP, CTX),
        check_vma=False,
    )
```

```python
import functools
import math

import jax
import jax.numpy as jnp
import numpy as np
from jax import lax
from jax.experimental import pallas as pl
from jax.experimental.pallas import tpu as pltpu
from jax.sharding import Mesh, PartitionSpec as P

ROPE = 64
QK = 128
SCALE = (QK + ROPE) ** -0.5
LOG2E = math.log2(math.e)
DEAD = -1e30
DP = ("z", "x", "yh")
PEERS = ("z", "yh")
CTX = ("yl", "core")
STAT_ROWS = 16
SLOTS = 4
VMEM = pl.BlockSpec(memory_space=pltpu.VMEM)
SMEM = pl.BlockSpec(memory_space=pltpu.SMEM)
ANY = pl.BlockSpec(memory_space=pl.ANY)


def product(a, b, dim_a, dim_b):
    return lax.dot_general(
        a, b, (((dim_a,), (dim_b,)), ((), ())), preferred_element_type=jnp.float32
    )


def swap(block, axis):
    return lax.ppermute(block, axis, [(0, 1), (1, 0)])


def call(kernel, name, out_shape, in_specs, scratch=(), out_specs=None, vmem=24, work=0):
    return pl.pallas_call(
        kernel,
        in_specs=in_specs,
        out_specs=jax.tree.map(lambda _: VMEM, out_shape) if out_specs is None else out_specs,
        out_shape=out_shape,
        scratch_shapes=list(scratch),
        compiler_params=pltpu.CompilerParams(vmem_limit_bytes=vmem << 20),
        cost_estimate=pl.CostEstimate(flops=work, bytes_accessed=work, transcendentals=0),
        name=name,
    )


def pack_kernel(up_ref, weight_ref, *refs):
    out_refs, sems = refs[:-1], refs[-1]
    owned, lat, head = up_ref.shape
    width = weight_ref.shape[1]
    copies = []
    for o in range(owned):
        pairs = [(weight_ref.at[pl.ds(o * head, head), :], out_refs[o].at[:, pl.ds(0, width)])]
        for k in range(lat // head):
            pairs.append(
                (
                    up_ref.at[o, pl.ds(k * head, head), :],
                    out_refs[o].at[:, pl.ds(width + k * head, head)],
                )
            )
        for src, dst in pairs:
            copies.append(pltpu.make_async_copy(src, dst, sems.at[len(copies)]))
    for copy in copies:
        copy.start()
    for copy in copies:
        copy.wait()


def pack(ups, weight):
    owned, lat, head = ups.shape
    shape = jax.ShapeDtypeStruct((head, weight.shape[1] + lat), jnp.bfloat16)
    ups = pltpu.with_memory_space_constraint(ups, pltpu.HBM)
    weight = pltpu.with_memory_space_constraint(weight, pltpu.HBM)
    sems = pltpu.SemaphoreType.DMA((owned * (1 + lat // head),))
    return call(
        pack_kernel, "pack", [shape] * owned, [ANY] * 2, [sems], out_specs=[ANY] * owned, vmem=1
    )(ups, weight)


def load_kernel(cache_ref, query_ref, out_cache_ref, out_query_ref, sems):
    rows = cache_ref.shape[0]
    copies = [pltpu.make_async_copy(query_ref, out_query_ref, sems.at[rows])]
    for row in range(rows):
        copies.append(
            pltpu.make_async_copy(cache_ref.at[row], out_cache_ref.at[row], sems.at[row])
        )
    for copy in copies:
        copy.start()
    for copy in copies:
        copy.wait()


def load(cache, queries):
    rows = cache.shape[0]
    cache = pltpu.with_memory_space_constraint(cache, pltpu.HBM)
    queries = pltpu.with_memory_space_constraint(queries, pltpu.HBM)
    return call(
        load_kernel,
        "load",
        [pltpu.VMEM(cache.shape, cache.dtype), pltpu.VMEM(queries.shape, queries.dtype)],
        [ANY] * 2,
        [pltpu.SemaphoreType.DMA((rows + 1,))],
        out_specs=[VMEM, VMEM],
        vmem=1,
        work=12 << 20,
    )(cache, queries)


def split_logsum(logsum):
    high = logsum.astype(jnp.bfloat16).astype(jnp.float32)
    middle = (logsum - high).astype(jnp.bfloat16).astype(jnp.float32)
    return [high, middle, logsum - high - middle]


def stat_block(logsums, width):
    parts = [part for logsum in logsums for part in split_logsum(logsum)]
    parts.append(jnp.zeros((STAT_ROWS - len(parts), parts[0].shape[1]), jnp.float32))
    block = jnp.concatenate(parts, axis=0)
    return jnp.concatenate([block, jnp.zeros((STAT_ROWS, width - block.shape[1]), jnp.float32)], axis=1)


def attend_kernel(lat, place_ref, length_ref, *refs):
    query_parts, (cache_ref, mine_ref, theirs_ref, query_ref, score_ref, weight_ref) = refs[:-6], refs[-6:]
    rows, block, _ = query_parts[0].shape
    heads = block * len(query_parts)
    span = cache_ref.shape[2]
    context, core = place_ref[0], place_ref[1]
    for k, part in enumerate(query_parts):
        first = pl.multiple_of((context ^ k) * block, block)
        for row in range(rows):
            query_ref[row, pl.ds(first, block), :] = part[row]

    positions = lax.broadcasted_iota(jnp.int32, (1, span), 1) + context * span

    def score(row):
        scores = product(query_ref[row], cache_ref[row], 1, 0)
        scores = jnp.where(positions < length_ref[row], scores, DEAD)
        score_ref[row % 2] = scores
        return jnp.max(scores, axis=1, keepdims=True)

    def weigh(row, peak):
        weights = jnp.exp2((score_ref[row % 2] - peak) * (SCALE * LOG2E))
        weight_ref[row % 2] = weights.astype(jnp.bfloat16)
        return jnp.sum(weights, axis=1, keepdims=True)

    half = lat // 2
    logsums = []

    def mix(row, peak, total):
        mixed = product(weight_ref[row % 2], cache_ref[row, :lat], 1, 1)
        mixed = (mixed / total).astype(jnp.bfloat16).astype(jnp.float32)
        low, high = mixed[:, :half], mixed[:, half:]
        place = slice(row * heads, (row + 1) * heads)
        mine_ref[place, :] = jnp.where(core == 0, low, high).astype(jnp.bfloat16)
        theirs_ref[place, :] = jnp.where(core == 0, high, low).astype(jnp.bfloat16)
        logsum = peak * SCALE + jnp.log(total)
        logsums.append(jnp.broadcast_to(logsum, (heads, heads)).T[0:1])

    peak = score(0)
    for row in range(rows):
        total = weigh(row, peak)
        following = score(row + 1) if row + 1 < rows else None
        mix(row, peak, total)
        peak = following
    stats = stat_block(logsums, half).astype(jnp.bfloat16)
    mine_ref[rows * heads :, :] = stats
    theirs_ref[rows * heads :, :] = stats


def attend(places, lengths, query_parts, cache, lat):
    rows, block, width = query_parts[0].shape
    heads = block * len(query_parts)
    span = cache.shape[2]
    shape = jax.ShapeDtypeStruct((rows * heads + STAT_ROWS, lat // 2), jnp.bfloat16)
    cache = pltpu.with_memory_space_constraint(cache, pltpu.VMEM)
    return call(
        functools.partial(attend_kernel, lat),
        "attend",
        [shape, shape],
        [SMEM, SMEM] + [VMEM] * (len(query_parts) + 1),
        [
            pltpu.VMEM((rows, heads, width), jnp.bfloat16),
            pltpu.VMEM((2, heads, span), jnp.float32),
            pltpu.VMEM((2, heads, span), jnp.bfloat16),
        ],
    )(places, lengths, *query_parts, cache)


def merge_states(rows, heads, refs):
    stats = [ref[rows * heads :, :heads].astype(jnp.float32) for ref in refs]
    shares, merged_logsums = [], []
    for row in range(rows):
        logsums = [sum(s[3 * row + k : 3 * row + k + 1] for k in range(3)) for s in stats]
        peak = functools.reduce(jnp.maximum, logsums)
        factors = [jnp.exp(v - peak) for v in logsums]
        total = functools.reduce(jnp.add, factors)
        shares += [f / total for f in factors]
        merged_logsums.append(peak + jnp.log(total))
    shares.append(jnp.zeros((heads - len(shares), heads), jnp.float32))
    shares = jnp.concatenate(shares, axis=0).T
    merged = []
    for row in range(rows):
        terms = []
        for c, ref in enumerate(refs):
            column = row * len(refs) + c
            values = ref[row * heads : (row + 1) * heads, :].astype(jnp.float32)
            terms.append(shares[:, column : column + 1] * values)
        merged.append(sum(terms).astype(jnp.bfloat16))
    return merged, merged_logsums


def merge_kernel(rows, heads, a_ref, b_ref, out_ref):
    merged, logsums = merge_states(rows, heads, (a_ref, b_ref))
    for row in range(rows):
        out_ref[row * heads : (row + 1) * heads, :] = merged[row]
    out_ref[rows * heads :, :] = stat_block(logsums, out_ref.shape[1]).astype(jnp.bfloat16)


def merge(a, b, rows, heads):
    shape = jax.ShapeDtypeStruct(a.shape, jnp.bfloat16)
    return call(functools.partial(merge_kernel, rows, heads), "merge", shape, [VMEM, VMEM])(a, b)


def finish_kernel(rows, heads, owned, sizes, a_ref, b_ref, out_ref):
    merged, _ = merge_states(rows, heads, (a_ref, b_ref))
    merged = jnp.concatenate(merged, axis=0)
    _, x, yh = sizes
    column = lax.broadcasted_iota(jnp.int32, (1, rows * heads), 1)
    row, head = column // heads, column % heads
    own, head = head % owned, head // owned
    side, head = head % yh, head // yh
    across, deep = head % x, head // x
    target = (((deep * yh + side) * x + across) * owned + own) * rows + row
    lines = lax.broadcasted_iota(jnp.int32, (rows * heads, 1), 0)
    order = jnp.where(lines == target, 1.0, 0.0).astype(jnp.bfloat16)
    out_ref[...] = product(order, merged, 1, 0).astype(jnp.bfloat16)


def finish(a, b, rows, heads, owned, sizes):
    shape = jax.ShapeDtypeStruct((rows * heads, a.shape[1]), jnp.bfloat16)
    kernel = functools.partial(finish_kernel, rows, heads, owned, sizes)
    return call(kernel, "finish", shape, [VMEM] * 2)(a, b)


def project_lines(lines, pieces, width):
    heads_out = []
    for rows, tile in zip(lines, pieces):
        head = tile.shape[0]
        up = [tile[:, j : j + head] for j in range(width, tile.shape[1], head)]
        heads_out.append(product(rows, jnp.concatenate(up, axis=0), 1, 0).astype(jnp.bfloat16))
    weight = jnp.concatenate([tile[:, :width] for tile in pieces], axis=0)
    return product(jnp.concatenate(heads_out, axis=1), weight, 1, 0)


def near_kernel(rows, owned, width, place_ref, mine_ref, theirs_ref, *refs):
    tiles, (sum_ref, far_ref, sorted_ref) = refs[:-3], refs[-3:]
    core, here = place_ref[1], place_ref[2]
    half = mine_ref.shape[1]
    slots = sum_ref.shape[0]
    peers = slots // SLOTS
    count = mine_ref.shape[0] // (peers * rows)
    target = lax.broadcasted_iota(jnp.int32, (sorted_ref.shape[0], 1), 0)
    slot, target = target % SLOTS, target // SLOTS
    holder, group = target % peers, target // peers
    source = jnp.where(slot < rows, (holder * count + group) * rows + slot, -1)
    columns = lax.broadcasted_iota(jnp.int32, (1, mine_ref.shape[0]), 1)
    select = jnp.where(columns == source, 1.0, 0.0).astype(jnp.bfloat16)
    mine, theirs = mine_ref[...], theirs_ref[...]
    low, high = jnp.where(core == 0, mine, theirs), jnp.where(core == 0, theirs, mine)
    sorted_ref[:, :half] = product(select, low, 1, 0).astype(jnp.bfloat16)
    sorted_ref[:, half:] = product(select, high, 1, 0).astype(jnp.bfloat16)
    ring = count // owned

    def lines(distance, o):
        first = ((here + distance) % ring * owned + o) * slots
        return sorted_ref[pl.ds(pl.multiple_of(first, slots), slots), :]

    result = None
    for k, distance in enumerate((0, ring - 1, 1)):
        pieces = tiles[k * owned : (k + 1) * owned]
        term = project_lines([lines(distance, o) for o in range(owned)], pieces, width)
        result = term if result is None else result + term
    sum_ref[...] = result
    for o in range(owned):
        far_ref[o * slots : (o + 1) * slots, :] = lines(2, o)


def project_near(places, mine, theirs, tiles, peers, rows, owned, width):
    count = mine.shape[0] // (peers * rows)
    slots = peers * SLOTS
    lat = 2 * mine.shape[1]
    return call(
        functools.partial(near_kernel, rows, owned, width),
        "project_near",
        [
            jax.ShapeDtypeStruct((slots, width), jnp.float32),
            jax.ShapeDtypeStruct((owned * slots, lat), jnp.bfloat16),
        ],
        [SMEM] + [VMEM] * (2 + len(tiles)),
        [pltpu.VMEM((count * slots, lat), jnp.bfloat16)],
    )(places, mine, theirs, *tiles)


def far_kernel(rows, width, sum_ref, line_ref, *refs):
    tiles, out_ref = refs[:-1], refs[-1]
    slots = sum_ref.shape[0]
    lines = [line_ref[o * slots : (o + 1) * slots, :] for o in range(len(tiles))]
    result = (sum_ref[...] + project_lines(lines, tiles, width)).astype(jnp.bfloat16)
    for d in range(out_ref.shape[0]):
        out_ref[d] = result[d * SLOTS : d * SLOTS + rows, :]


def project_far(near, lines, tiles, peers, rows, width):
    return call(
        functools.partial(far_kernel, rows, width),
        "project_far",
        jax.ShapeDtypeStruct((peers, rows, width), jnp.bfloat16),
        [VMEM] * (2 + len(tiles)),
    )(near, lines, *tiles)


def total_kernel(part_ref, out_ref):
    parts = [part_ref[k].astype(jnp.float32) for k in range(part_ref.shape[0])]
    while len(parts) > 1:
        parts = [a + b for a, b in zip(parts[::2], parts[1::2])]
    out_ref[...] = parts[0].astype(jnp.bfloat16)


def total(parts):
    shape = jax.ShapeDtypeStruct(parts.shape[1:], jnp.bfloat16)
    return call(total_kernel, "total", shape, [VMEM])(parts)


def from_x(block, distance):
    size = lax.axis_size("x")
    return lax.ppermute(block, "x", [(i, (i + distance) % size) for i in range(size)])


def shards(queries, cache, lengths, ups, weight):
    rows = queries.shape[0]
    owned, lat, _ = ups.shape
    sizes = tuple(lax.axis_size(a) for a in DP)
    heads = math.prod(sizes) * owned
    peers = math.prod(lax.axis_size(a) for a in PEERS)
    places = jnp.stack([lax.axis_index(CTX), lax.axis_index("core"), lax.axis_index("x")])

    across = swap(queries, "yl")
    partner = swap(queries, "core")
    own = pack(ups, weight)
    behind, ahead = from_x(own[0], 1), from_x(own[1], -1)

    cache, held = load(jnp.swapaxes(cache, 1, 2), queries)
    query_parts = [held, partner, across, swap(across, "core")]
    mine, theirs = attend(places, lengths, query_parts, cache, lat)
    behind_too, ahead_too = from_x(own[1], 1), from_x(own[0], -1)
    theirs, behind, ahead = lax.optimization_barrier((theirs, behind, ahead))
    state = merge(mine, swap(theirs, "core"), rows, heads)
    tiles = [*own, behind, behind_too, ahead_too, ahead, from_x(behind, 1), from_x(ahead, -1)]
    latents = finish(state, swap(state, "yl"), rows, heads, owned, sizes)

    latents = latents.reshape(peers, -1, lat // 2)
    latents = lax.all_to_all(latents, PEERS, 0, 0, tiled=True)
    latents = latents.reshape(rows * heads, lat // 2)
    width = weight.shape[1]
    theirs = swap(latents, "core")
    near, lines = project_near(places, latents, theirs, tiles[:-2], peers, rows, owned, width)
    partial = project_far(near, lines, tiles[-2:], peers, rows, width)
    partial = lax.all_to_all(partial, PEERS, 0, 0, tiled=True)
    return total(partial)


def solution(mesh):
    inner = Mesh(mesh.devices.reshape(8, 4, 2, 2, 2), DP + CTX)
    return jax.shard_map(
        shards,
        mesh=inner,
        in_specs=(
            P(DP, CTX, None),
            P(DP, CTX, None),
            P(DP),
            P(DP, None, None),
            P(DP, CTX),
        ),
        out_specs=P(DP, CTX),
        check_vma=False,
    )
```
